256 devices in a mesh: region: 64 (over z, y, x_hi), orb: 4 (over x_lo, core).
Axes of the slice: x: 4 (x_hi: 2, x_lo: 2; x = x_hi * 2 + x_lo), y: 4, z: 8, core: 2. Of those that a mesh axis runs over, the one named last changes fastest.
Arguments:
- orbitals: bfloat16 [2048, 49152], P(('orb', 'region')), may hold values from -1 to 1
- point_region: int32 [49152], replicated, may hold values from 0 to 63, as said below
- coulomb: bfloat16 [64, 4, 768, 768], P('region'), may hold values from 0.049804688 to 1
- pair_mask: int32 [64, 3], P('region'), may hold values 0 or 1
Outputs:
- exchange_out: float32 [2048, 49152], P('orb', 'region')
The draws below stay inside these ranges and needn't reach their ends.
Inputs may be any that keep to these rules, and one draw needn't show every extreme that they name: `point_region`: each of the 64 regions holds exactly 768 points, and every aligned brick of 128 consecutive points lies in one region.
All inputs are finite; a program needn't handle non-finite values. No bound on the sum of `pair_mask` on one device may be relied on, other than what follows from the above.
Results may differ from the reference program's by a relative error of at most 0.0025.
Values may be sent and summed in bfloat16 or wider, within the bound.
No kernel may reach another device: no remote copies, remote signals or barrier semaphores. Data moves between devices by JAX's collectives and lax.ppermute only.
A program may use at most 128 MiB of HBM per device.

```python
import math
import jax
import jax.numpy as jnp
from jax import lax

NOCC = 2048
PT_DEV = 768
TILE = 128
NFAR = 3
NREG = 64
NPTS = 49152


def draw_point_region(key, part):
    key = jax.random.fold_in(key, 7)
    brick_labels = jnp.arange(NPTS // TILE, dtype=jnp.int32) // (PT_DEV // TILE)
    shuffled = jax.random.permutation(key, brick_labels)
    return jnp.repeat(shuffled, TILE)


def place_ends(array, rng, low, top_value):
    place = [jax.random.randint(jax.random.fold_in(rng, axis), (), 0, length) for axis, length in enumerate(array.shape)]
    widest = array.shape.index(max(array.shape))
    neighbour = place[:widest] + [(place[widest] + 1) % array.shape[widest]] + place[widest + 1:]
    return array.at[tuple(place)].set(low).at[tuple(neighbour)].set(top_value)


def steps_of(key, shape, shards, least, top_value):
    gain = 1.0
    for dim, shards_of in shards:
        steps = jax.random.uniform(jax.random.fold_in(jax.random.fold_in(key, 6), dim), (shards_of,), jnp.float32, least / len(shards), top_value / len(shards))
        gain = gain * jnp.repeat(jnp.exp(steps), shape[dim] // shards_of).reshape((-1,) + (1,) * (len(shape) - 1 - dim))
    return gain


def centred(rng, shape, width, reach, split=(), kind=jnp.bfloat16):
    entries = jax.random.normal(rng, shape, jnp.float32) * width
    if len(split) > 0:
        entries = steps_of(rng, shape, split, -0.22, 0.18) * entries
    return jnp.clip(entries, min=-reach, max=reach).astype(kind)


def setup_inputs(seed: int = 0) -> dict:
    arg_keys = jax.random.split(jax.random.key(seed), 5)
    orbitals = centred(arg_keys[0], (NOCC, NPTS), 0.15, 1.0, ((0, 256),))
    point_region = draw_point_region(jax.random.fold_in(arg_keys[4], 71), 0)
    coulomb = jnp.clip(jnp.exp(math.log(1.0) - 2.9996462 * jax.random.uniform(arg_keys[2], (NREG, NFAR + 1, PT_DEV, PT_DEV), jnp.float32) ** steps_of(arg_keys[2], (NREG, NFAR + 1, PT_DEV, PT_DEV), ((0, 64),), -0.2, 0.2)), 0.049804688, 1.0).astype(jnp.bfloat16)
    pair_mask = place_ends((jax.random.randint(arg_keys[3], (NREG, NFAR), 0, 4) < 3).astype(jnp.int32), jax.random.fold_in(arg_keys[3], 1), 0, 1)
    return dict(orbitals=orbitals, point_region=point_region, coulomb=coulomb, pair_mask=pair_mask)


def reference(orbitals, point_region, coulomb, pair_mask):
    order = jnp.argsort(point_region, stable=True)
    grouped = orbitals[:, order]
    blocks = grouped.reshape(NOCC, NREG, PT_DEV).transpose(1, 0, 2)
    weights = jnp.concatenate([jnp.ones((NREG, 1), jnp.int32), pair_mask], axis=1)

    def one_region(index):
        own = blocks[index]
        forward = jnp.zeros((NOCC, PT_DEV), jnp.float32)
        backs = []
        for offset in range(NFAR + 1):
            other = blocks[(index + offset) % NREG]
            gram = lax.dot_general(own, other, (((0,), (0,)), ((), ())), preferred_element_type=jnp.float32)
            scale = weights[index, offset].astype(jnp.bfloat16)
            product = (gram * coulomb[index, offset].astype(jnp.float32)).astype(jnp.bfloat16) * scale
            forward = forward + lax.dot_general(other, product, (((1,), (1,)), ((), ())), preferred_element_type=jnp.float32)
            if offset > 0:
                backs.append(jnp.dot(own, product, preferred_element_type=jnp.float32))
        return forward, jnp.stack(backs)

    forward, backs = lax.map(one_region, jnp.arange(NREG, dtype=jnp.int32))
    total = forward
    for offset in range(1, NFAR + 1):
        total = total + jnp.roll(backs[:, offset - 1], offset, axis=0)
    return (-0.25 * total).transpose(1, 0, 2).reshape(NOCC, NPTS)
```

```python
import jax
import jax.numpy as jnp
from jax import lax
from jax.sharding import PartitionSpec as P

TILE = 128


def moved(array, regions, chips=0, cores=0):
    size, orbs = lax.axis_size("region"), lax.axis_size("orb")
    pairs = [
        (r * orbs + o, (r + regions) % size * orbs + (o ^ (2 * chips + cores)))
        for r in range(size)
        for o in range(orbs)
    ]
    return lax.ppermute(array, ("region", "orb"), pairs)


def cross(left, right):
    return lax.dot_general(
        left, right, (((0,), (0,)), ((), ())), preferred_element_type=jnp.float32
    )


def onto_rows(orbs, product):
    return lax.dot_general(
        orbs, product, (((1,), (1,)), ((), ())), preferred_element_type=jnp.float32
    )


def onto_columns(orbs, product):
    return jnp.dot(orbs, product, preferred_element_type=jnp.float32)


def per_device(orbitals, point_region, coulomb, pair_mask):
    count = orbitals.shape[0]
    npoints = orbitals.shape[1]
    bricks = npoints // TILE
    core = lax.axis_index("orb") % 2
    half = coulomb.shape[2] // 2
    weights = pair_mask[0].astype(jnp.bfloat16)

    rows = lax.dynamic_slice_in_dim(coulomb[0], core * half, half, axis=1)
    away = jnp.stack([rows[1] * weights[0], rows[3] * weights[2]])
    behind = moved(away, 1, chips=1)

    brick_region = point_region.reshape(bricks, TILE)[:, 0]
    order = jnp.argsort(brick_region, stable=True)
    grouped = jnp.take(orbitals.reshape(count, bricks, TILE), order, axis=1).reshape(count, npoints)
    own = lax.all_to_all(grouped, "region", split_axis=1, concat_axis=0, tiled=True)
    prev = moved(own, 1)
    ahead = moved(own, -2)

    def on_chip(block):
        return jnp.concatenate([block, moved(block, 0, cores=1)], axis=0)

    def screened(left, right, block):
        mine = lax.dynamic_slice_in_dim(left, core * half, half, axis=1)
        partial = cross(mine, right)
        gram = partial + moved(partial.astype(jnp.bfloat16), 0, chips=1).astype(jnp.float32)
        product = (gram * block.astype(jnp.float32)).astype(jnp.bfloat16)
        other = moved(product, 0, cores=1)
        first = core == 0
        return jnp.concatenate(
            [jnp.where(first, product, other), jnp.where(first, other, product)], axis=0
        )

    own_chip, prev_chip, ahead_chip = on_chip(own), on_chip(prev), on_chip(ahead)
    self_pair = screened(own_chip, own_chip, rows[0])
    prev_own = screened(prev_chip, own_chip, behind[0])
    prev_ahead = screened(prev_chip, ahead_chip, behind[1])
    own_ahead = screened(own_chip, ahead_chip, rows[2] * weights[1])

    to_prev = onto_rows(own, prev_own) + onto_rows(ahead, prev_ahead)
    to_ahead = onto_columns(own, own_ahead) + onto_columns(prev, prev_ahead)
    from_next = moved(to_prev.astype(jnp.bfloat16), -1)
    from_back = moved(to_ahead.astype(jnp.bfloat16), 2)
    total = onto_rows(own, self_pair) + onto_rows(ahead, own_ahead) + onto_columns(prev, prev_own)
    total = total + from_next.astype(jnp.float32) + from_back.astype(jnp.float32)
    return -0.25 * total


def solution(mesh):
    in_specs = (P(("orb", "region"), None), P(), P("region", None, None, None), P("region", None))
    out_specs = P("orb", "region")
    return jax.shard_map(
        per_device, mesh=mesh, in_specs=in_specs, out_specs=out_specs, check_vma=False
    )
```

```python
import functools

import jax
import jax.numpy as jnp
from jax import lax
from jax.experimental import pallas as pl
from jax.experimental.pallas import tpu as pltpu
from jax.sharding import PartitionSpec as P

TILE = 128


def moved(array, regions, chips=0, cores=0):
    size, orbs = lax.axis_size("region"), lax.axis_size("orb")
    pairs = [
        (r * orbs + o, (r + regions) % size * orbs + (o ^ (2 * chips + cores)))
        for r in range(size)
        for o in range(orbs)
    ]
    return lax.ppermute(array, ("region", "orb"), pairs)


def call(kernel, scalars, operands, in_specs, out_specs, out_shape, name):
    return pl.pallas_call(
        kernel,
        grid_spec=pltpu.PrefetchScalarGridSpec(
            num_scalar_prefetch=1, grid=(1,), in_specs=in_specs, out_specs=out_specs
        ),
        out_shape=out_shape,
        compiler_params=pltpu.CompilerParams(vmem_limit_bytes=24 * 2**20),
        cost_estimate=pl.CostEstimate(flops=0, bytes_accessed=0, transcendentals=0),
        name=name,
    )(scalars, *operands)


def whole(shape):
    return pl.BlockSpec(shape, lambda i, s: (0,) * len(shape))


def first_rows(left, right):
    return lax.dot_general(
        left, right, (((0,), (0,)), ((), ())), preferred_element_type=jnp.float32
    )


def onto_rows(orbs, product):
    return lax.dot_general(
        orbs, product, (((1,), (1,)), ((), ())), preferred_element_type=jnp.float32
    )


def onto_columns(orbs, product):
    return jnp.dot(orbs, product, preferred_element_type=jnp.float32)


def lanes(scalars, width):
    core = scalars[0]
    return (
        pl.ds(pl.multiple_of(core * width, TILE), width),
        pl.ds(pl.multiple_of((1 - core) * width, TILE), width),
    )


def gram_kernel(count, weight, scalars, *refs):
    lefts, rights, rest, out = refs[:count], refs[count : 2 * count], refs[2 * count : -1], refs[-1]
    total = sum(first_rows(left[...], right[...]) for left, right in zip(lefts, rights))
    if weight is None:
        out[...] = total
        return
    *partial, block = rest
    if partial:
        total = total + partial[0][...]
    total = (total * block[...].reshape(out.shape).astype(jnp.float32)).astype(jnp.bfloat16)
    if weight:
        total = total * scalars[weight].astype(jnp.bfloat16)
    out[...] = total


def gram(scalars, lefts, rights, partial=None, block=None, k=0):
    orbs, points = lefts[0].shape
    half = points // 2
    mine = pl.BlockSpec((orbs, half), lambda i, s: (0, s[0]))
    operands = [*lefts, *rights]
    specs = [mine] * len(lefts) + [whole((orbs, points))] * len(rights)
    if partial is not None:
        operands.append(partial)
        specs.append(whole((half, points)))
    if block is not None:
        operands.append(block)
        if block.ndim == 4:
            specs.append(pl.BlockSpec((1, 1, half, points), lambda i, s: (0, k, s[0], 0)))
        else:
            specs.append(pl.BlockSpec((half, points), lambda i, s: (k, 0)))
    weight = None if block is None else k if block.ndim == 4 else 0
    return call(
        functools.partial(gram_kernel, len(lefts), weight),
        scalars,
        operands,
        specs,
        whole((half, points)),
        jax.ShapeDtypeStruct((half, points), jnp.float32 if block is None else jnp.bfloat16),
        "gram",
    )


def away_kernel(scalars, one, three, out):
    half = out.shape[0] // 2
    out[:half] = one[0, 0] * scalars[1].astype(out.dtype)
    out[half:] = three[0, 0] * scalars[3].astype(out.dtype)


def away(scalars, coulomb):
    points = coulomb.shape[3]

    def block(k):
        return pl.BlockSpec((1, 1, points // 2, points), lambda i, s: (0, k, s[0], 0))

    return call(
        away_kernel,
        scalars,
        (coulomb, coulomb),
        [block(1), block(3)],
        whole((points, points)),
        jax.ShapeDtypeStruct((points, points), coulomb.dtype),
        "away",
    )


def to_prev_kernel(scalars, own, ahead, po, po_too, pa, pa_too, out):
    for part, by_own, by_ahead in zip(lanes(scalars, po.shape[0]), (po, po_too), (pa, pa_too)):
        total = onto_rows(own[...], by_own[...]) + onto_rows(ahead[...], by_ahead[...])
        out[:, part] = total.astype(out.dtype)


def to_ahead_kernel(scalars, own, prev, oa, oa_too, pa, pa_too, out):
    mine, other = lanes(scalars, oa.shape[0])
    total = onto_columns(own[:, mine], oa[...]) + onto_columns(own[:, other], oa_too[...])
    total += onto_columns(prev[:, mine], pa[...]) + onto_columns(prev[:, other], pa_too[...])
    out[...] = total.astype(out.dtype)


def stay_kernel(scalars, own, ahead, prev, oo, oo_too, oa, oa_too, po, po_too, out):
    mine, other = lanes(scalars, po.shape[0])
    out[...] = onto_columns(prev[:, mine], po[...]) + onto_columns(prev[:, other], po_too[...])
    for part, by_own, by_ahead in zip((mine, other), (oo, oo_too), (oa, oa_too)):
        out[:, part] += onto_rows(own[...], by_own[...]) + onto_rows(ahead[...], by_ahead[...])


def applied(kernel, scalars, orbs, products, dtype):
    shape = orbs[0].shape
    operands = (*orbs, *(p for pair in products for p in pair))
    return call(
        kernel,
        scalars,
        operands,
        [whole(o.shape) for o in operands],
        whole(shape),
        jax.ShapeDtypeStruct(shape, dtype),
        kernel.__name__,
    )


def per_device(orbitals, point_region, coulomb, pair_mask):
    count = orbitals.shape[0]
    npoints = orbitals.shape[1]
    bricks = npoints // TILE
    core = lax.axis_index("orb") % 2
    scalars = jnp.concatenate([core[None].astype(jnp.int32), pair_mask[0]])

    brick_region = point_region.reshape(bricks, TILE)[:, 0]
    order = jnp.argsort(brick_region, stable=True)
    grouped = jnp.take(orbitals.reshape(count, bricks, TILE), order, axis=1).reshape(count, npoints)
    own = lax.all_to_all(grouped, "region", split_axis=1, concat_axis=0, tiled=True)
    def beside(block):
        return moved(block, 0, cores=1)

    own_x = moved(own, 0, chips=1)
    prev_x = moved(own, 1, chips=1)
    ahead = moved(own, -2)
    own_s = beside(own)

    later, _ = lax.optimization_barrier((scalars, own))
    sent = away(later, coulomb)
    prev_x, own_x, ahead, sent = lax.optimization_barrier((prev_x, own_x, ahead, sent))
    behind = moved(sent, 1, chips=1)
    prev = moved(prev_x, 0, chips=1)
    ahead_x = moved(own_x, -2)
    own_xs, prev_xs, ahead_s = beside(own_x), beside(prev_x), beside(ahead)
    all_own = (own, own_s, own_x, own_xs)
    oo = gram(scalars, all_own, all_own, None, coulomb, 0)
    po = gram(scalars, (prev_x, prev_xs), (own_x, own_xs))
    oa = gram(scalars, (own, own_s), (ahead, ahead_s))
    ahead_x, prev, oo, po, oa = lax.optimization_barrier((ahead_x, prev, oo, po, oa))
    prev_s, ahead_xs = beside(prev), beside(ahead_x)
    oa = gram(scalars, (own_x, own_xs), (ahead_x, ahead_xs), oa, coulomb, 2)
    behind, oa = lax.optimization_barrier((behind, oa))
    po = gram(scalars, (prev, prev_s), (own, own_s), po, behind, 0)
    pa = gram(
        scalars,
        (prev, prev_s, prev_x, prev_xs),
        (ahead, ahead_s, ahead_x, ahead_xs),
        None,
        behind,
        1,
    )

    po, pa, oa, oo = ((p, beside(p)) for p in (po, pa, oa, oo))
    to_prev = applied(to_prev_kernel, scalars, (own_x, ahead_x), (po, pa), jnp.bfloat16)
    from_next = moved(to_prev, -1, chips=1)
    to_ahead = applied(to_ahead_kernel, scalars, (own, prev), (oa, pa), jnp.bfloat16)
    from_back = moved(to_ahead, 2)
    stay = applied(stay_kernel, scalars, (own, ahead, prev), (oo, oa, po), jnp.float32)
    return -0.25 * (stay + from_next.astype(jnp.float32) + from_back.astype(jnp.float32))


def solution(mesh):
    in_specs = (P(("orb", "region"), None), P(), P("region", None, None, None), P("region", None))
    out_specs = P("orb", "region")
    return jax.shard_map(
        per_device, mesh=mesh, in_specs=in_specs, out_specs=out_specs, check_vma=False
    )
```

```python
import functools

import jax
import jax.numpy as jnp
from jax import lax
from jax.experimental import pallas as pl
from jax.experimental.pallas import tpu as pltpu
from jax.sharding import PartitionSpec as P

TILE = 128


def moved(array, regions, chips=0, cores=0):
    size, orbs = lax.axis_size("region"), lax.axis_size("orb")
    pairs = [
        (r * orbs + o, (r + regions) % size * orbs + (o ^ (2 * chips + cores)))
        for r in range(size)
        for o in range(orbs)
    ]
    return lax.ppermute(array, ("region", "orb"), pairs)


def call(kernel, scalars, operands, in_specs, out_specs, out_shape, name):
    return pl.pallas_call(
        kernel,
        grid_spec=pltpu.PrefetchScalarGridSpec(
            num_scalar_prefetch=1, grid=(1,), in_specs=in_specs, out_specs=out_specs
        ),
        out_shape=out_shape,
        compiler_params=pltpu.CompilerParams(vmem_limit_bytes=24 * 2**20),
        cost_estimate=pl.CostEstimate(flops=0, bytes_accessed=0, transcendentals=0),
        name=name,
    )(scalars, *operands)


def whole(shape):
    return pl.BlockSpec(shape, lambda i, s: (0,) * len(shape))


def first_rows(left, right):
    return lax.dot_general(
        left, right, (((0,), (0,)), ((), ())), preferred_element_type=jnp.float32
    )


def onto_rows(orbs, product):
    return lax.dot_general(
        orbs, product, (((1,), (1,)), ((), ())), preferred_element_type=jnp.float32
    )


def onto_columns(orbs, product):
    return jnp.dot(orbs, product, preferred_element_type=jnp.float32)


def lanes(scalars, width):
    core = scalars[0]
    return (
        pl.ds(pl.multiple_of(core * width, TILE), width),
        pl.ds(pl.multiple_of((1 - core) * width, TILE), width),
    )


def gram_kernel(count, weight, scalars, *refs):
    lefts, rights, rest, out = refs[:count], refs[count : 2 * count], refs[2 * count : -1], refs[-1]
    total = sum(first_rows(left[...], right[...]) for left, right in zip(lefts, rights))
    if weight is None:
        out[...] = total
        return
    *partial, block = rest
    if partial:
        total = total + partial[0][...]
    total = (total * block[...].reshape(out.shape).astype(jnp.float32)).astype(jnp.bfloat16)
    if weight:
        total = total * scalars[weight].astype(jnp.bfloat16)
    out[...] = total


def gram(scalars, lefts, rights, partial=None, block=None, k=0):
    orbs, points = lefts[0].shape
    half = points // 2
    mine = pl.BlockSpec((orbs, half), lambda i, s: (0, s[0]))
    operands = [*lefts, *rights]
    specs = [mine] * len(lefts) + [whole((orbs, points))] * len(rights)
    if partial is not None:
        operands.append(partial)
        specs.append(whole((half, points)))
    weight = None
    if block is not None:
        operands.append(block)
        if block.ndim == 4:
            weight = k
            specs.append(pl.BlockSpec((1, 1, half, points), lambda i, s: (0, k, s[0], 0)))
        else:
            weight = 0
            specs.append(pl.BlockSpec((half, points), lambda i, s: (k, 0)))
    return call(
        functools.partial(gram_kernel, len(lefts), weight),
        scalars,
        operands,
        specs,
        whole((half, points)),
        jax.ShapeDtypeStruct((half, points), jnp.float32 if block is None else jnp.bfloat16),
        "gram",
    )


def away_kernel(scalars, one, three, out):
    half = out.shape[0] // 2
    out[:half] = one[0, 0] * scalars[1].astype(out.dtype)
    out[half:] = three[0, 0] * scalars[3].astype(out.dtype)


def away(scalars, coulomb):
    points = coulomb.shape[3]
    coulomb = pltpu.with_memory_space_constraint(coulomb, pltpu.HBM)

    def block(k):
        return pl.BlockSpec((1, 1, points // 2, points), lambda i, s: (0, k, s[0], 0))

    return call(
        away_kernel,
        scalars,
        (coulomb, coulomb),
        [block(1), block(3)],
        whole((points, points)),
        jax.ShapeDtypeStruct((points, points), coulomb.dtype),
        "away",
    )


def to_prev_kernel(scalars, own, ahead, po, po_too, pa, pa_too, out):
    for part, by_own, by_ahead in zip(lanes(scalars, po.shape[0]), (po, po_too), (pa, pa_too)):
        total = onto_rows(own[...], by_own[...]) + onto_rows(ahead[...], by_ahead[...])
        out[:, part] = total.astype(out.dtype)


def to_ahead_kernel(scalars, own, prev, oa, oa_too, pa, pa_too, out):
    mine, other = lanes(scalars, oa.shape[0])
    total = onto_columns(own[:, mine], oa[...]) + onto_columns(own[:, other], oa_too[...])
    total += onto_columns(prev[:, mine], pa[...]) + onto_columns(prev[:, other], pa_too[...])
    out[...] = total.astype(out.dtype)


def stay_kernel(scalars, own, ahead, prev, oo, oo_too, oa, oa_too, po, po_too, out):
    mine, other = lanes(scalars, po.shape[0])
    out[...] = onto_columns(prev[:, mine], po[...]) + onto_columns(prev[:, other], po_too[...])
    for part, by_own, by_ahead in zip((mine, other), (oo, oo_too), (oa, oa_too)):
        out[:, part] += onto_rows(own[...], by_own[...]) + onto_rows(ahead[...], by_ahead[...])


def applied(kernel, scalars, orbs, products, dtype):
    shape = orbs[0].shape
    operands = (*orbs, *(p for pair in products for p in pair))
    return call(
        kernel,
        scalars,
        operands,
        [whole(o.shape) for o in operands],
        whole(shape),
        jax.ShapeDtypeStruct(shape, dtype),
        kernel.__name__,
    )


def group_kernel(scalars, order, orbitals, out):
    bricks = out.shape[2] // TILE
    for region in range(out.shape[0]):
        for brick in range(bricks):
            start = pl.multiple_of(order[region * bricks + brick] * TILE, TILE)
            out[region, :, brick * TILE : (brick + 1) * TILE] = orbitals[:, pl.ds(start, TILE)]


def grouped_by_region(scalars, order, orbitals, points):
    shape = (orbitals.shape[1] // points, orbitals.shape[0], points)
    return pl.pallas_call(
        group_kernel,
        grid_spec=pltpu.PrefetchScalarGridSpec(
            num_scalar_prefetch=2,
            grid=(1,),
            in_specs=[pl.BlockSpec(orbitals.shape, lambda i, s, o: (0, 0))],
            out_specs=pl.BlockSpec(shape, lambda i, s, o: (0, 0, 0)),
        ),
        out_shape=jax.ShapeDtypeStruct(shape, orbitals.dtype),
        compiler_params=pltpu.CompilerParams(vmem_limit_bytes=24 * 2**20),
        cost_estimate=pl.CostEstimate(flops=0, bytes_accessed=0, transcendentals=0),
        name="group",
    )(scalars, order, orbitals)


def per_device(orbitals, point_region, coulomb, pair_mask):
    bricks = orbitals.shape[1] // TILE
    core = lax.axis_index("orb") % 2
    scalars = jnp.concatenate([core[None].astype(jnp.int32), pair_mask[0]])

    brick_region = point_region.reshape(bricks, TILE)[:, 0]
    region = jnp.arange(bricks, dtype=jnp.int32)
    before = (brick_region[None, :] < brick_region[:, None]) | (
        (brick_region[None, :] == brick_region[:, None]) & (region[None, :] < region[:, None])
    )
    rank = jnp.sum(before.astype(jnp.int32), axis=1)
    order = jnp.sum(jnp.where(rank[:, None] == region[None, :], region[:, None], 0), axis=0)
    grouped = grouped_by_region(scalars, order, orbitals, coulomb.shape[2])
    own = lax.all_to_all(grouped, "region", split_axis=0, concat_axis=0, tiled=True)
    own = own.reshape(-1, coulomb.shape[2])

    def beside(block):
        return moved(block, 0, cores=1)

    own_x = moved(own, 0, chips=1)
    prev_x = moved(own, 1, chips=1)
    ahead = moved(own, -2)
    own_s = beside(own)

    later, _ = lax.optimization_barrier((scalars, own))
    sent = away(later, coulomb)
    prev_x, own_x, ahead, sent = lax.optimization_barrier((prev_x, own_x, ahead, sent))
    behind = moved(sent, 1, chips=1)
    prev = moved(prev_x, 0, chips=1)
    ahead_x = moved(own_x, -2)
    own_xs, prev_xs, ahead_s = beside(own_x), beside(prev_x), beside(ahead)
    all_own = (own, own_s, own_x, own_xs)
    oo = gram(scalars, all_own, all_own, None, coulomb, 0)
    po = gram(scalars, (prev_x, prev_xs), (own_x, own_xs))
    oa = gram(scalars, (own, own_s), (ahead, ahead_s))
    ahead_x, prev, oo, po, oa = lax.optimization_barrier((ahead_x, prev, oo, po, oa))
    prev_s, ahead_xs = beside(prev), beside(ahead_x)
    oa = gram(scalars, (own_x, own_xs), (ahead_x, ahead_xs), oa, coulomb, 2)
    behind, oa = lax.optimization_barrier((behind, oa))
    pa = gram(
        scalars,
        (prev, prev_s, prev_x, prev_xs),
        (ahead, ahead_s, ahead_x, ahead_xs),
        None,
        behind,
        1,
    )
    po = gram(scalars, (prev, prev_s), (own, own_s), po, behind, 0)
    pa, oa, oo = ((p, beside(p)) for p in (pa, oa, oo))
    to_ahead = applied(to_ahead_kernel, scalars, (own, prev), (oa, pa), jnp.bfloat16)
    from_back = moved(to_ahead, 2)
    po = po, beside(po)
    to_prev = applied(to_prev_kernel, scalars, (own_x, ahead_x), (po, pa), jnp.bfloat16)
    from_next = moved(to_prev, -1, chips=1)
    stay = applied(stay_kernel, scalars, (own, ahead, prev), (oo, oa, po), jnp.float32)
    return -0.25 * (stay + from_next.astype(jnp.float32) + from_back.astype(jnp.float32))


def solution(mesh):
    in_specs = (P(("orb", "region"), None), P(), P("region", None, None, None), P("region", None))
    out_specs = P("orb", "region")
    return jax.shard_map(
        per_device, mesh=mesh, in_specs=in_specs, out_specs=out_specs, check_vma=False
    )
```

```python
import functools

import jax
import jax.numpy as jnp
from jax import lax
from jax.experimental import pallas as pl
from jax.experimental.pallas import tpu as pltpu
from jax.sharding import PartitionSpec as P

TILE = 128


def moved(array, regions, chips=0, cores=0):
    size, orbs = lax.axis_size("region"), lax.axis_size("orb")
    pairs = [
        (r * orbs + o, (r + regions) % size * orbs + (o ^ (2 * chips + cores)))
        for r in range(size)
        for o in range(orbs)
    ]
    return lax.ppermute(array, ("region", "orb"), pairs)


def call(kernel, scalars, operands, in_specs, out_specs, out_shape, name):
    return pl.pallas_call(
        kernel,
        grid_spec=pltpu.PrefetchScalarGridSpec(
            num_scalar_prefetch=1, grid=(1,), in_specs=in_specs, out_specs=out_specs
        ),
        out_shape=out_shape,
        compiler_params=pltpu.CompilerParams(vmem_limit_bytes=24 * 2**20),
        cost_estimate=pl.CostEstimate(flops=0, bytes_accessed=0, transcendentals=0),
        name=name,
    )(scalars, *operands)


def whole(shape):
    return pl.BlockSpec(shape, lambda i, s: (0,) * len(shape))


def first_rows(left, right):
    return lax.dot_general(
        left, right, (((0,), (0,)), ((), ())), preferred_element_type=jnp.float32
    )


def onto_rows(orbs, product):
    return lax.dot_general(
        orbs, product, (((1,), (1,)), ((), ())), preferred_element_type=jnp.float32
    )


def onto_columns(orbs, product):
    return jnp.dot(orbs, product, preferred_element_type=jnp.float32)


def lanes(scalars, width):
    core = scalars[0]
    return (
        pl.ds(pl.multiple_of(core * width, TILE), width),
        pl.ds(pl.multiple_of((1 - core) * width, TILE), width),
    )


def gram_kernel(count, weight, scalars, *refs):
    lefts, rights, rest, out = refs[:count], refs[count : 2 * count], refs[2 * count : -1], refs[-1]
    total = sum(first_rows(left[...], right[...]) for left, right in zip(lefts, rights))
    if weight is None:
        out[...] = total + rest[0][...] if rest else total
        return
    *partial, block = rest
    if partial:
        total = total + partial[0][...]
    total = (total * block[...].reshape(out.shape).astype(jnp.float32)).astype(jnp.bfloat16)
    if weight:
        total = total * scalars[weight].astype(jnp.bfloat16)
    out[...] = total


def gram(scalars, lefts, rights, partial=None, block=None, k=0):
    orbs, points = lefts[0].shape
    half = points // 2
    mine = pl.BlockSpec((orbs, half), lambda i, s: (0, s[0]))
    operands = [*lefts, *rights]
    specs = [mine] * len(lefts) + [whole((orbs, points))] * len(rights)
    if partial is not None:
        operands.append(partial)
        specs.append(whole((half, points)))
    if block is not None:
        operands.append(block)
        specs.append(pl.BlockSpec((1, 1, half, points), lambda i, s: (0, k, s[0], 0)))
    weight = None if block is None else k
    return call(
        functools.partial(gram_kernel, len(lefts), weight),
        scalars,
        operands,
        specs,
        whole((half, points)),
        jax.ShapeDtypeStruct((half, points), jnp.float32 if block is None else jnp.bfloat16),
        "gram",
    )


def screen_kernel(scalars, gram, block, out):
    out[...] = (gram[...] * block[...].astype(jnp.float32)).astype(out.dtype)


def screened(scalars, gram, blocks, k):
    return call(
        screen_kernel,
        scalars,
        (gram, blocks),
        [whole(gram.shape), pl.BlockSpec(gram.shape, lambda i, s: (k, 0))],
        whole(gram.shape),
        jax.ShapeDtypeStruct(gram.shape, jnp.bfloat16),
        "screen",
    )


def away_kernel(scalars, one, three, out):
    half = out.shape[0] // 2
    out[:half] = one[0, 0] * scalars[1].astype(out.dtype)
    out[half:] = three[0, 0] * scalars[3].astype(out.dtype)


def away(scalars, coulomb):
    points = coulomb.shape[3]
    coulomb = pltpu.with_memory_space_constraint(coulomb, pltpu.HBM)

    def block(k):
        return pl.BlockSpec((1, 1, points // 2, points), lambda i, s: (0, k, s[0], 0))

    return call(
        away_kernel,
        scalars,
        (coulomb, coulomb),
        [block(1), block(3)],
        whole((points, points)),
        jax.ShapeDtypeStruct((points, points), coulomb.dtype),
        "away",
    )


def to_prev_kernel(scalars, own, ahead, po, po_too, pa, pa_too, out):
    for part, by_own, by_ahead in zip(lanes(scalars, po.shape[0]), (po, po_too), (pa, pa_too)):
        total = onto_rows(own[...], by_own[...]) + onto_rows(ahead[...], by_ahead[...])
        out[:, part] = total.astype(out.dtype)


def to_ahead_kernel(scalars, own, prev, oa, oa_too, pa, pa_too, out):
    mine, other = lanes(scalars, oa.shape[0])
    total = onto_columns(own[:, mine], oa[...]) + onto_columns(own[:, other], oa_too[...])
    total += onto_columns(prev[:, mine], pa[...]) + onto_columns(prev[:, other], pa_too[...])
    out[...] = total.astype(out.dtype)


def stay_kernel(scalars, own, ahead, prev, oo, oo_too, oa, oa_too, po, po_too, out):
    mine, other = lanes(scalars, po.shape[0])
    out[...] = onto_columns(prev[:, mine], po[...]) + onto_columns(prev[:, other], po_too[...])
    for part, by_own, by_ahead in zip((mine, other), (oo, oo_too), (oa, oa_too)):
        out[:, part] += onto_rows(own[...], by_own[...]) + onto_rows(ahead[...], by_ahead[...])


def applied(kernel, scalars, operands, shape, dtype):
    return call(
        kernel,
        scalars,
        operands,
        [whole(o.shape) for o in operands],
        whole(shape),
        jax.ShapeDtypeStruct(shape, dtype),
        kernel.__name__,
    )


def group_kernel(scalars, order, orbitals, out):
    bricks = out.shape[2] // TILE
    for region in range(out.shape[0]):
        for brick in range(bricks):
            start = pl.multiple_of(order[region * bricks + brick] * TILE, TILE)
            out[region, :, brick * TILE : (brick + 1) * TILE] = orbitals[:, pl.ds(start, TILE)]


def grouped_by_region(scalars, order, orbitals, points):
    shape = (orbitals.shape[1] // points, orbitals.shape[0], points)
    return pl.pallas_call(
        group_kernel,
        grid_spec=pltpu.PrefetchScalarGridSpec(
            num_scalar_prefetch=2,
            grid=(1,),
            in_specs=[pl.BlockSpec(orbitals.shape, lambda i, s, o: (0, 0))],
            out_specs=pl.BlockSpec(shape, lambda i, s, o: (0, 0, 0)),
        ),
        out_shape=jax.ShapeDtypeStruct(shape, orbitals.dtype),
        compiler_params=pltpu.CompilerParams(vmem_limit_bytes=24 * 2**20),
        cost_estimate=pl.CostEstimate(flops=0, bytes_accessed=0, transcendentals=0),
        name="group",
    )(scalars, order, orbitals)


def per_device(orbitals, point_region, coulomb, pair_mask):
    bricks = orbitals.shape[1] // TILE
    core = lax.axis_index("orb") % 2
    scalars = jnp.concatenate([core[None].astype(jnp.int32), pair_mask[0]])

    brick_region = point_region.reshape(bricks, TILE)[:, 0]
    region = jnp.arange(bricks, dtype=jnp.int32)
    before = (brick_region[None, :] < brick_region[:, None]) | (
        (brick_region[None, :] == brick_region[:, None]) & (region[None, :] < region[:, None])
    )
    rank = jnp.sum(before.astype(jnp.int32), axis=1)
    order = jnp.sum(jnp.where(rank[:, None] == region[None, :], region[:, None], 0), axis=0)
    grouped = grouped_by_region(scalars, order, orbitals, coulomb.shape[2])
    own = lax.all_to_all(grouped, "region", split_axis=0, concat_axis=0, tiled=True)
    own = own.reshape(-1, coulomb.shape[2])

    def beside(block):
        return moved(block, 0, cores=1)

    own_x = moved(own, 0, chips=1)
    prev_x = moved(own, 1, chips=1)
    ahead = moved(own, -2)
    own_s = beside(own)

    later, _ = lax.optimization_barrier((scalars, own))
    sent = away(later, coulomb)
    prev_x, sent = lax.optimization_barrier((prev_x, sent))
    behind = moved(sent, 1, chips=1)
    prev = moved(prev_x, 0, chips=1)
    ahead_x = moved(own_x, -2)
    own_xs, prev_xs, ahead_s = beside(own_x), beside(prev_x), beside(ahead)
    all_own = (own, own_s, own_x, own_xs)
    oo = gram(scalars, all_own, all_own, None, coulomb, 0)
    po = gram(scalars, (prev_x, prev_xs), (own_x, own_xs))
    oa = gram(scalars, (own, own_s), (ahead, ahead_s))
    ahead_x, prev, oo = lax.optimization_barrier((ahead_x, prev, own_xs))[:2] + (oo,)
    prev_s, ahead_xs = beside(prev), beside(ahead_x)
    oa = gram(scalars, (own_x, own_xs), (ahead_x, ahead_xs), oa, coulomb, 2)
    pa = gram(scalars, (prev, prev_s, prev_x, prev_xs), (ahead, ahead_s, ahead_x, ahead_xs))
    po = gram(scalars, (prev, prev_s), (own, own_s), po)
    shape = own.shape
    behind, pa, po, _ = lax.optimization_barrier((behind, pa, po, oa))
    shape = own.shape
    oo, oa = ((p, beside(p)) for p in (oo, oa))
    pa = screened(scalars, pa, behind, 1)
    po = screened(scalars, po, behind, 0)
    pa, po = ((p, beside(p)) for p in (pa, po))
    to_ahead = applied(to_ahead_kernel, scalars, (own, prev, *oa, *pa), shape, jnp.bfloat16)
    from_back = moved(to_ahead, 2)
    to_prev = applied(to_prev_kernel, scalars, (own_x, ahead_x, *po, *pa), shape, jnp.bfloat16)
    from_next = moved(to_prev, -1, chips=1)
    stay = applied(stay_kernel, scalars, (own, ahead, prev, *oo, *oa, *po), shape, jnp.float32)
    return -0.25 * (stay + from_next.astype(jnp.float32) + from_back.astype(jnp.float32))


def solution(mesh):
    in_specs = (P(("orb", "region"), None), P(), P("region", None, None, None), P("region", None))
    out_specs = P("orb", "region")
    return jax.shard_map(
        per_device, mesh=mesh, in_specs=in_specs, out_specs=out_specs, check_vma=False
    )
```

```python
import functools

import jax
import jax.numpy as jnp
from jax import lax
from jax.experimental import pallas as pl
from jax.experimental.pallas import tpu as pltpu
from jax.sharding import PartitionSpec as P

TILE = 128


def moved(array, regions, chips=0, cores=0):
    size, orbs = lax.axis_size("region"), lax.axis_size("orb")
    pairs = [
        (r * orbs + o, (r + regions) % size * orbs + (o ^ (2 * chips + cores)))
        for r in range(size)
        for o in range(orbs)
    ]
    return lax.ppermute(array, ("region", "orb"), pairs)


def call(kernel, scalars, operands, in_specs, out_specs, out_shape, name):
    return pl.pallas_call(
        kernel,
        grid_spec=pltpu.PrefetchScalarGridSpec(
            num_scalar_prefetch=1, grid=(1,), in_specs=in_specs, out_specs=out_specs
        ),
        out_shape=out_shape,
        compiler_params=pltpu.CompilerParams(vmem_limit_bytes=24 * 2**20),
        cost_estimate=pl.CostEstimate(flops=0, bytes_accessed=0, transcendentals=0),
        name=name,
    )(scalars, *operands)


def whole(shape):
    return pl.BlockSpec(shape, lambda i, s: (0,) * len(shape))


def first_rows(left, right):
    return lax.dot_general(
        left, right, (((0,), (0,)), ((), ())), preferred_element_type=jnp.float32
    )


def onto_rows(orbs, product):
    return lax.dot_general(
        orbs, product, (((1,), (1,)), ((), ())), preferred_element_type=jnp.float32
    )


def onto_columns(orbs, product):
    return jnp.dot(orbs, product, preferred_element_type=jnp.float32)


def lanes(scalars, width):
    core = scalars[0]
    return (
        pl.ds(pl.multiple_of(core * width, TILE), width),
        pl.ds(pl.multiple_of((1 - core) * width, TILE), width),
    )


def gram_kernel(count, weight, scalars, *refs):
    lefts, rights, rest, out = refs[:count], refs[count : 2 * count], refs[2 * count : -1], refs[-1]
    total = sum(first_rows(left[...], right[...]) for left, right in zip(lefts, rights))
    if weight is None:
        out[...] = total + rest[0][...] if rest else total
        return
    *partial, block = rest
    if partial:
        total = total + partial[0][...]
    total = (total * block[...].reshape(out.shape).astype(jnp.float32)).astype(jnp.bfloat16)
    if weight:
        total = total * scalars[weight].astype(jnp.bfloat16)
    out[...] = total


def gram(scalars, lefts, rights, partial=None, block=None, k=0):
    orbs, points = lefts[0].shape
    half = points // 2
    mine = pl.BlockSpec((orbs, half), lambda i, s: (0, s[0]))
    operands = [*lefts, *rights]
    specs = [mine] * len(lefts) + [whole((orbs, points))] * len(rights)
    if partial is not None:
        operands.append(partial)
        specs.append(whole((half, points)))
    if block is not None:
        operands.append(block)
        specs.append(pl.BlockSpec((1, 1, half, points), lambda i, s: (0, k, s[0], 0)))
    weight = None if block is None else k
    return call(
        functools.partial(gram_kernel, len(lefts), weight),
        scalars,
        operands,
        specs,
        whole((half, points)),
        jax.ShapeDtypeStruct((half, points), jnp.float32 if block is None else jnp.bfloat16),
        "gram",
    )


def screen_kernel(scalars, gram, block, out):
    out[...] = (gram[...] * block[...].astype(jnp.float32)).astype(out.dtype)


def screened(scalars, gram, blocks, k):
    return call(
        screen_kernel,
        scalars,
        (gram, blocks),
        [whole(gram.shape), pl.BlockSpec(gram.shape, lambda i, s: (k, 0))],
        whole(gram.shape),
        jax.ShapeDtypeStruct(gram.shape, jnp.bfloat16),
        "screen",
    )


def away_kernel(scalars, one, three, out):
    half = out.shape[0] // 2
    out[:half] = one[0, 0] * scalars[1].astype(out.dtype)
    out[half:] = three[0, 0] * scalars[3].astype(out.dtype)


def away(scalars, coulomb):
    points = coulomb.shape[3]
    coulomb = pltpu.with_memory_space_constraint(coulomb, pltpu.HBM)

    def block(k):
        return pl.BlockSpec((1, 1, points // 2, points), lambda i, s: (0, k, s[0], 0))

    return call(
        away_kernel,
        scalars,
        (coulomb, coulomb),
        [block(1), block(3)],
        whole((points, points)),
        jax.ShapeDtypeStruct((points, points), coulomb.dtype),
        "away",
    )


def to_prev_kernel(scalars, own, ahead, po, po_too, pa, pa_too, out):
    for part, by_own, by_ahead in zip(lanes(scalars, po.shape[0]), (po, po_too), (pa, pa_too)):
        total = onto_rows(own[...], by_own[...]) + onto_rows(ahead[...], by_ahead[...])
        out[:, part] = total.astype(out.dtype)


def to_ahead_kernel(scalars, own, prev, oa, oa_too, pa, pa_too, out):
    mine, other = lanes(scalars, oa.shape[0])
    total = onto_columns(own[:, mine], oa[...]) + onto_columns(own[:, other], oa_too[...])
    total += onto_columns(prev[:, mine], pa[...]) + onto_columns(prev[:, other], pa_too[...])
    out[...] = total.astype(out.dtype)


def stay_kernel(scalars, own, ahead, prev, oo, oo_too, oa, oa_too, po, po_too, out):
    mine, other = lanes(scalars, po.shape[0])
    out[...] = onto_columns(prev[:, mine], po[...]) + onto_columns(prev[:, other], po_too[...])
    for part, by_own, by_ahead in zip((mine, other), (oo, oo_too), (oa, oa_too)):
        out[:, part] += onto_rows(own[...], by_own[...]) + onto_rows(ahead[...], by_ahead[...])


def applied(kernel, scalars, operands, shape, dtype):
    return call(
        kernel,
        scalars,
        operands,
        [whole(o.shape) for o in operands],
        whole(shape),
        jax.ShapeDtypeStruct(shape, dtype),
        kernel.__name__,
    )


def group_kernel(order, orbitals, out):
    bricks = out.shape[2] // TILE
    for region in range(out.shape[0]):
        for brick in range(bricks):
            start = pl.multiple_of(order[region * bricks + brick] * TILE, TILE)
            out[region, :, brick * TILE : (brick + 1) * TILE] = orbitals[:, pl.ds(start, TILE)]


def grouped_by_region(order, orbitals, points):
    shape = (orbitals.shape[1] // points, orbitals.shape[0], points)
    return pl.pallas_call(
        group_kernel,
        grid_spec=pltpu.PrefetchScalarGridSpec(
            num_scalar_prefetch=1,
            grid=(1,),
            in_specs=[pl.BlockSpec(orbitals.shape, lambda i, o: (0, 0))],
            out_specs=pl.BlockSpec(shape, lambda i, o: (0, 0, 0)),
        ),
        out_shape=jax.ShapeDtypeStruct(shape, orbitals.dtype),
        compiler_params=pltpu.CompilerParams(vmem_limit_bytes=24 * 2**20),
        cost_estimate=pl.CostEstimate(flops=0, bytes_accessed=0, transcendentals=0),
        name="group",
    )(order, orbitals)


def per_device(orbitals, point_region, coulomb, pair_mask):
    bricks = orbitals.shape[1] // TILE
    core = lax.axis_index("orb") % 2
    scalars = jnp.concatenate([core[None].astype(jnp.int32), pair_mask[0]])

    brick_region = point_region.reshape(bricks, TILE)[:, 0]
    region = jnp.arange(bricks, dtype=jnp.int32)
    before = (brick_region[None, :] < brick_region[:, None]) | (
        (brick_region[None, :] == brick_region[:, None]) & (region[None, :] < region[:, None])
    )
    rank = jnp.sum(before.astype(jnp.int32), axis=1)
    order = jnp.sum(jnp.where(rank[:, None] == region[None, :], region[:, None], 0), axis=0)
    grouped = grouped_by_region(order, orbitals, coulomb.shape[2])
    own = lax.all_to_all(grouped, "region", split_axis=0, concat_axis=0, tiled=True)
    own = own.reshape(-1, coulomb.shape[2])

    def beside(block):
        return moved(block, 0, cores=1)

    own_x = moved(own, 0, chips=1)
    prev_x = moved(own, 1, chips=1)
    ahead = moved(own, -2)
    own_s = beside(own)

    later, _ = lax.optimization_barrier((scalars, own))
    sent = away(later, coulomb)
    prev_x, sent = lax.optimization_barrier((prev_x, sent))
    behind = moved(sent, 1, chips=1)
    prev = moved(prev_x, 0, chips=1)
    ahead_x = moved(own_x, -2)
    own_xs, prev_xs, ahead_s = beside(own_x), beside(prev_x), beside(ahead)
    all_own = (own, own_s, own_x, own_xs)
    oo = gram(scalars, all_own, all_own, None, coulomb, 0)
    po = gram(scalars, (prev_x, prev_xs), (own_x, own_xs))
    oa = gram(scalars, (own, own_s), (ahead, ahead_s))
    ahead_x, prev, oo = lax.optimization_barrier((ahead_x, prev, own_xs))[:2] + (oo,)
    prev_s, ahead_xs = beside(prev), beside(ahead_x)
    oa = gram(scalars, (own_x, own_xs), (ahead_x, ahead_xs), oa, coulomb, 2)
    pa = gram(scalars, (prev, prev_s, prev_x, prev_xs), (ahead, ahead_s, ahead_x, ahead_xs))
    po = gram(scalars, (prev, prev_s), (own, own_s), po)
    shape = own.shape
    behind, pa, po, _ = lax.optimization_barrier((behind, pa, po, oa))
    shape = own.shape
    oo, oa = ((p, beside(p)) for p in (oo, oa))
    pa = screened(scalars, pa, behind, 1)
    po = screened(scalars, po, behind, 0)
    pa, po = ((p, beside(p)) for p in (pa, po))
    to_ahead = applied(to_ahead_kernel, scalars, (own, prev, *oa, *pa), shape, jnp.bfloat16)
    from_back = moved(to_ahead, 2)
    to_prev = applied(to_prev_kernel, scalars, (own_x, ahead_x, *po, *pa), shape, jnp.bfloat16)
    from_next = moved(to_prev, -1, chips=1)
    stay = applied(stay_kernel, scalars, (own, ahead, prev, *oo, *oa, *po), shape, jnp.float32)
    return -0.25 * (stay + from_next.astype(jnp.float32) + from_back.astype(jnp.float32))


def solution(mesh):
    in_specs = (P(("orb", "region"), None), P(), P("region", None, None, None), P("region", None))
    out_specs = P("orb", "region")
    return jax.shard_map(
        per_device, mesh=mesh, in_specs=in_specs, out_specs=out_specs, check_vma=False
    )
```
